128 devices in a mesh: kpt: 16 (over y, x_lo, core), aux: 8 (over z, x_hi).
Axes of the slice: x: 4 (x_hi: 2, x_lo: 2; x = x_hi * 2 + x_lo), y: 4, z: 4, core: 2. Of those that a mesh axis runs over, the one named last changes fastest.
Arguments:
- amplitudes: bfloat16 [16, 2, 384, 384], P('kpt'), may hold values from -4 to 4
- integrals: bfloat16 [16, 2, 384, 384], P('kpt'), may hold values from -12 to 12
- left_factor: bfloat16 [16, 16, 16, 384, 384], P('kpt', None, 'aux'), may hold values from -0.109375 to 0.109375
- right_factor: bfloat16 [16, 16, 16, 384, 384], P('kpt', None, 'aux'), may hold values from -0.109375 to 0.109375
- pair_energy: float32 [2], replicated, may hold values from -2 to -0.6
- virt_energy: float32 [16, 384], replicated, may hold values from 0.3 to 3
- kconserve: int32 [16, 16, 16], replicated, may hold values from 0 to 15, as said below
Outputs:
- updated_amplitudes: bfloat16 [16, 2, 384, 384], P('kpt')
The draws below stay inside these ranges and needn't reach their ends.
Inputs may be any that keep to these rules, and one draw needn't show every extreme that they name: `kconserve`: for fixed first two indices the map over the third index is a permutation of the 16 momenta, with table[i, j, table[i, j, a]] = a; the table is an additive momentum law on relabelled momenta.
All inputs are finite; a program needn't handle non-finite values.
Results may differ from the reference program's by a relative error of at most 0.0055.
Values may be sent and summed in bfloat16 or wider, within the bound.
A program may use at most 64 MiB of HBM per device.

```python
import jax
import jax.numpy as jnp
from jax import lax

NV = 384
PAIRS = 2
ITERS = 2
NK = 16
NAUX = 16


def draw_kconserve(key, part):
    key = jax.random.fold_in(key, 7)
    labels = jax.random.permutation(key, NK).astype(jnp.int32)
    inverse = jnp.zeros((NK,), jnp.int32).at[labels].set(jnp.arange(NK, dtype=jnp.int32))
    target = (labels[:, None, None] + labels[None, :, None] - labels[None, None, :]) % NK
    return inverse[target]


def block_scale(rng, extent, cuts, smallest, high):
    loudness = 1.0
    for dim, blocks in cuts:
        heights = jax.random.uniform(jax.random.fold_in(jax.random.fold_in(rng, 6), dim), (blocks,), jnp.float32, smallest / len(cuts), high / len(cuts))
        loudness = loudness * jnp.repeat(jnp.exp(heights), extent[dim] // blocks).reshape((-1,) + (1,) * (len(extent) - 1 - dim))
    return loudness


def centred(rng, shape, spread, reach, split=(), held_as=jnp.bfloat16):
    gain = block_scale(rng, shape, split, -0.22, 0.18) if split else 1.0
    array = jax.random.normal(rng, shape, jnp.float32) * spread * gain
    return jnp.minimum(jnp.maximum(array, -reach), reach).astype(held_as)


def setup_inputs(seed: int = 0) -> dict:
    arg_keys = jax.random.split(jax.random.key(seed), 8)
    return {
        "amplitudes": centred(arg_keys[0], (NK, PAIRS, NV, NV), 0.5, 4.0, ((0, 16),)),
        "integrals": centred(arg_keys[1], (NK, PAIRS, NV, NV), 2.0, 12.0, ((0, 16),)),
        "left_factor": centred(arg_keys[2], (NK, NK, NAUX, NV, NV), (NV * 8) ** -0.5, 0.109375, ((0, 16), (2, 8))),
        "right_factor": centred(arg_keys[3], (NK, NK, NAUX, NV, NV), (NV * 8) ** -0.5, 0.109375, ((0, 16), (2, 8))),
        "pair_energy": jnp.clip(jax.random.uniform(arg_keys[4], (PAIRS,), jnp.float32, -2.0, -0.6), -2.0, -0.6),
        "virt_energy": jnp.clip(jax.random.uniform(arg_keys[5], (NK, NV), jnp.float32, 0.3, 3.0), 0.3, 3.0),
        "kconserve": draw_kconserve(jax.random.fold_in(arg_keys[7], 71), 0),
    }


def reference(amplitudes, integrals, left_factor, right_factor, pair_energy, virt_energy, kconserve):
    partner = kconserve[0, 0]
    energy_b = virt_energy[partner]
    denominator = pair_energy[None, :, None, None] - virt_energy[:, None, :, None] - energy_b[:, None, None, :]
    integral_f = integrals.astype(jnp.float32)

    def ladder(current):
        def one_momentum(ka):
            def advance(totals, kc):
                amp_block = current[kc].astype(jnp.float32)
                right_panel = right_factor[ka, kc].astype(jnp.float32)
                halfway = jnp.einsum('pcd,lbd->lpcb', amp_block, right_panel, precision=lax.Precision.HIGHEST)
                halfway = lax.optimization_barrier(halfway.astype(jnp.bfloat16)).astype(jnp.float32)
                left_panel = left_factor[ka, kc].astype(jnp.float32)
                return totals + jnp.einsum('lac,lpcb->pab', left_panel, halfway, precision=lax.Precision.HIGHEST), None
            start_sum = jnp.zeros((PAIRS, NV, NV), jnp.float32)
            totals, unused = lax.scan(advance, start_sum, jnp.arange(NK, dtype=jnp.int32))
            return totals
        return lax.map(one_momentum, jnp.arange(NK, dtype=jnp.int32))

    current = amplitudes
    for repeat in range(ITERS):
        current = ((integral_f + ladder(current)) / denominator).astype(jnp.bfloat16)
    return current
```

```python
import functools

import jax
import jax.numpy as jnp
from jax import lax
from jax.experimental import pallas as pl
from jax.experimental.pallas import tpu as pltpu
from jax.sharding import PartitionSpec as P

ITERS = 2
MESH = pl.DeviceIdType.MESH
BF16, F32 = jnp.bfloat16, jnp.float32

NV, PAIRS, NK = 384, 2, 16
LOCAL_AUX = 2
CHUNK = NV // 8
PIECE = NV // 4
HALF = NV // 2

AUX = ((1, 0), (3, 0), (2, 0), (0, 1), (1, 1), (3, 1), (2, 1))
ORDER = ((0, 0), (0, 1), (2, 0), (1, 0), (3, 0), (2, 1), (1, 1), (3, 1))

TO_CORE = 0
QUARTER = 8
QUARTER_X = 9
ALONG_Z = 11
OWN_X = 17
OWN_Y = 19
RELAY_X = 27
RELAY_Y = 39
COPIES = 41


def kernel(
    amp_hbm, int_hbm, left_hbm, right_hbm, pair_ref, virt_ref, cons_ref,
    out_hbm,
    cur, left, right, own, half, acc, parts_out, parts_in, ints, den,
    send, recv, rs_send, rs_recv, ag_send, ag_recv, load, edge,
):
    kpt, aux = lax.axis_index("kpt"), lax.axis_index("aux")
    y, xl, core = kpt // 4, (kpt // 2) % 2, kpt % 2
    z, xh = aux // 2, aux % 2

    def device(dy=0, dx=0, dc=0, dz=0, dh=0):
        x = (2 * xh + xl + dx + 2 * dh) % 4
        return (
            (((y + dy) % 4) * 2 + x % 2) * 2 + (core + dc) % 2,
            ((z + dz) % 4) * 2 + x // 2,
        )

    def block(dy, dx):
        return (((y + dy) % 4) * 2 + (xl + dx) % 2) * 2 + core

    partners = [device(dc=1)]
    partners += [device(dy=1), device(dy=3), device(dy=2), device(dx=1), device(dx=3)]
    partners += [device(dz=dz, dh=dh) for dz, dh in AUX]
    barrier = pltpu.get_barrier_semaphore()
    for partner in partners:
        pl.semaphore_signal(barrier, inc=1, device_id=partner, device_id_type=MESH)

    def first_load():
        return pltpu.make_async_copy(amp_hbm.at[0], own.at[0], edge.at[0])

    def ints_load():
        rows = pl.ds(pl.multiple_of(aux * CHUNK, 16), CHUNK)
        return pltpu.make_async_copy(int_hbm.at[0, :, rows], ints, edge.at[1])

    def step_place(step):
        later = (step + 6) // 8
        third = (step + 1) % 3
        dx = (1 - later) * step + later * ((step + 1) // 3 - 1)
        dy = later * (2 - third % 2 + third // 2)
        return ((y + dy) % 4) * 2 + (xl + dx) % 2

    def panel_load(step, which):
        place = step_place(step) * 2
        source, target = ((left_hbm, left), (right_hbm, right))[which]
        return pltpu.make_async_copy(
            source.at[0, pl.ds(place, 2)], target.at[pl.ds(place, 2)], load.at[which, step]
        )

    first_load().start()

    def start_loads(step, unused):
        panel_load(step, 1).start()
        panel_load(step, 0).start()
        return unused

    lax.fori_loop(0, 8, start_loads, 0)
    ints_load().start()

    partner_row = cons_ref[0, 0, kpt]
    energy_b = virt_ref[pl.ds(partner_row, 1), :]
    energy_a = virt_ref[pl.ds(kpt, 1), :]
    row = lax.broadcasted_iota(jnp.int32, (CHUNK, NV), 0) + aux * CHUNK
    lane = lax.broadcasted_iota(jnp.int32, (CHUNK, NV), 1)
    column = jnp.sum(
        jnp.where(row == lane, jnp.broadcast_to(energy_a, (CHUNK, NV)), 0.0), axis=1, keepdims=True
    )
    for p in range(PAIRS):
        den[p] = (pair_ref[p] - column) - energy_b

    ints_load().wait()
    first_load().wait()
    pl.semaphore_wait(barrier, len(partners))

    def copy(it, number, place, start, size, target=None, source=None):
        rows = pl.ds(start if isinstance(start, int) else pl.multiple_of(start, 16), size)
        there = cur.at[it, place, :, rows]
        here = there if source is None else source.at[:, rows]
        return pltpu.make_async_remote_copy(
            src_ref=here, dst_ref=there,
            send_sem=send.at[it, number], recv_sem=recv.at[it, number],
            device_id=device(dc=1) if target is None else target, device_id_type=MESH,
        )

    def to_core(it, which, sibling=False):
        dy, dx = ORDER[which]
        place = block(dy, dx)
        if sibling:
            place = place + 1 - 2 * core
        return copy(it, TO_CORE + which, place, 0, NV)

    def quarter(it, receive=False):
        if receive:
            return copy(it, QUARTER, block(2, 0), z * PIECE, PIECE)
        return copy(it, QUARTER, block(0, 0), z * PIECE, PIECE, device(dy=2), own.at[it])

    def quarter_x(it, way, receive=False):
        start = z * PIECE + way * CHUNK
        target = device(dx=(1, 3)[way])
        return copy(it, QUARTER_X + way, block(2, 1 if receive else 0), start, CHUNK, target)

    def along_z(it, column, way, receive=False):
        dz = (1, 3, 2)[way]
        start = ((z + 4 - dz) % 4 if receive else z) * PIECE
        return copy(it, ALONG_Z + 3 * column + way, block(2, column), start, PIECE, device(dz=dz))

    def own_x(it, way, receive=False):
        if receive:
            return copy(it, OWN_X + way, block(0, 1), way * HALF, HALF)
        target = device(dx=(1, 3)[way])
        return copy(it, OWN_X + way, block(0, 0), way * HALF, HALF, target, own.at[it])

    def own_y(it, piece, way, receive=False):
        number = OWN_Y + 2 * piece + way
        if receive:
            return copy(it, number, block((3, 1)[way], 0), piece * PIECE, PIECE)
        target = device(dy=(1, 3)[way])
        return copy(it, number, block(0, 0), piece * PIECE, PIECE, target, own.at[it])

    def relay_x(it, piece, which, way, receive=False):
        number = RELAY_X + 4 * piece + 2 * which + way
        start = piece * PIECE + way * CHUNK
        target = device(dx=(1, 3)[way])
        return copy(it, number, block((3, 1)[which], 1 if receive else 0), start, CHUNK, target)

    def relay_y(it, way, receive=False):
        target = device(dy=(1, 3)[way])
        dy = (3, 1)[way] if receive else 0
        return copy(it, RELAY_Y + way, block(dy, 1), 3 * PIECE, PIECE, target)

    def aux_index(o, back=False):
        dz, dh = AUX[o]
        return device(dz=4 - dz if back else dz, dh=dh)[1]

    def rs_copy(it, o):
        dz, dh = AUX[o]
        return pltpu.make_async_remote_copy(
            src_ref=parts_out.at[it, o], dst_ref=parts_in.at[it, o],
            send_sem=rs_send.at[it, o], recv_sem=rs_recv.at[it, o],
            device_id=device(dz=dz, dh=dh), device_id_type=MESH,
        )

    def ag_copy(it, o, receive=False):
        dz, dh = AUX[o]
        index = aux_index(o, True) if receive else aux
        rows = pl.ds(pl.multiple_of(index * CHUNK, 16), CHUNK)
        return pltpu.make_async_remote_copy(
            src_ref=own.at[it + 1, :, rows], dst_ref=own.at[it + 1, :, rows],
            send_sem=ag_send.at[it, o], recv_sem=ag_recv.at[it, o],
            device_id=device(dz=dz, dh=dh), device_id_type=MESH,
        )

    def events(it, step):
        if step == 0:
            cur[it, block(0, 0)] = own[it]
            to_core(it, 0).start()
            quarter(it).start()
            for way in range(2):
                own_x(it, way).start()
            for piece in range(4):
                for way in range(2):
                    own_y(it, piece, way).start()
            acc[...] = jnp.zeros_like(acc)

        def take_piece(piece):
            for way in range(2):
                own_y(it, piece, way, True).wait_recv()
            if piece < 3:
                for which in range(2):
                    for way in range(2):
                        relay_x(it, piece, which, way).start()

        if step == 1:
            quarter(it, True).wait_recv()
            for way in range(2):
                quarter_x(it, way).start()
            for way in range(3):
                along_z(it, 0, way).start()
            for way in range(2):
                own_x(it, way, True).wait_recv()
            to_core(it, 1).start()
            for way in range(2):
                relay_y(it, way).start()
            take_piece(0)
        if step == 2:
            for way in range(2):
                quarter_x(it, way, True).wait_recv()
            for way in range(3):
                along_z(it, 1, way).start()
            take_piece(1)
            for way in range(3):
                along_z(it, 0, way, True).wait_recv()
            to_core(it, 2).start()
        if step == 3:
            take_piece(2)
            take_piece(3)
            to_core(it, 3).start()
            to_core(it, 4).start()
        if step == 5:
            for way in range(3):
                along_z(it, 1, way, True).wait_recv()
            to_core(it, 5).start()
        if step == 6:
            for piece in range(3):
                for which in range(2):
                    for way in range(2):
                        relay_x(it, piece, which, way, True).wait_recv()
            for way in range(2):
                relay_y(it, way, True).wait_recv()
            to_core(it, 6).start()
            to_core(it, 7).start()
        to_core(it, step, sibling=True).wait_recv()

    def close(it):
        for o in range(7):
            rows = pl.ds(pl.multiple_of(aux_index(o) * CHUNK, 16), CHUNK)
            for p in range(PAIRS):
                parts_out[it, o, p] = acc[rows, p * NV : (p + 1) * NV].astype(BF16)
            rs_copy(it, o).start()
        for o in range(7):
            rs_copy(it, o).wait_recv()
        rows = pl.ds(pl.multiple_of(aux * CHUNK, 16), CHUNK)
        for p in range(PAIRS):
            total = acc[rows, p * NV : (p + 1) * NV]
            for o in range(7):
                total = total + parts_in[it, o, p].astype(F32)
            own[it + 1, p, rows] = ((ints[p].astype(F32) + total) / den[p]).astype(BF16)
        for o in range(7):
            ag_copy(it, o).start()
        for o in range(7):
            ag_copy(it, o, True).wait_recv()

    def turn(number, unused):
        it, step = number // 8, number % 8
        for at in range(8):
            pl.when(step == at)(functools.partial(events, it, at))

        @pl.when(it == 0)
        def _():
            panel_load(step, 1).wait()
            panel_load(step, 0).wait()

        place = step_place(step) * 2
        for i in range(2):
            amp = cur[it, place + i].reshape(PAIRS * NV, NV)
            panel = right[place + i].reshape(LOCAL_AUX * NV, NV)
            product = lax.dot_general(
                amp, panel, (((1,), (1,)), ((), ())), preferred_element_type=F32
            ).astype(BF16)
            for l in range(LOCAL_AUX):
                for p in range(PAIRS):
                    half[(i * 2 + l) * NV : (i * 2 + l + 1) * NV, p * NV : (p + 1) * NV] = product[
                        p * NV : (p + 1) * NV, l * NV : (l + 1) * NV
                    ]
        panels = jnp.concatenate([left[place + i, l] for i in range(2) for l in range(2)], axis=1)
        acc[...] += jnp.dot(panels, half[...], preferred_element_type=F32)
        pl.when(step == 7)(functools.partial(close, it))
        return unused

    lax.fori_loop(0, 8 * ITERS, turn, 0)

    write = pltpu.make_async_copy(own.at[ITERS], out_hbm.at[0], edge.at[2])
    write.start()

    def drain(it, unused):
        for which in range(8):
            to_core(it, which).wait_send()
        quarter(it).wait_send()
        for way in range(2):
            quarter_x(it, way).wait_send()
            own_x(it, way).wait_send()
            relay_y(it, way).wait_send()
            for piece in range(4):
                own_y(it, piece, way).wait_send()
            for piece in range(3):
                for which in range(2):
                    relay_x(it, piece, which, way).wait_send()
        for column in range(2):
            for way in range(3):
                along_z(it, column, way).wait_send()
        for o in range(7):
            rs_copy(it, o).wait_send()
            ag_copy(it, o).wait_send()
        return unused

    lax.fori_loop(0, ITERS, drain, 0)
    write.wait()


def on_device(*args):
    anywhere = pl.BlockSpec(memory_space=pl.ANY)
    vmem = pl.BlockSpec(memory_space=pltpu.VMEM)
    smem = pl.BlockSpec(memory_space=pltpu.SMEM)
    dma = pltpu.SemaphoreType.DMA
    return pl.pallas_call(
        kernel,
        out_shape=jax.ShapeDtypeStruct((1, PAIRS, NV, NV), BF16),
        in_specs=[anywhere] * 4 + [smem, vmem, smem],
        out_specs=anywhere,
        scratch_shapes=[
            pltpu.VMEM((ITERS, NK, PAIRS, NV, NV), BF16),
            pltpu.VMEM((NK, LOCAL_AUX, NV, NV), BF16),
            pltpu.VMEM((NK, LOCAL_AUX, NV, NV), BF16),
            pltpu.VMEM((ITERS + 1, PAIRS, NV, NV), BF16),
            pltpu.VMEM((2 * LOCAL_AUX * NV, PAIRS * NV), BF16),
            pltpu.VMEM((NV, PAIRS * NV), F32),
            pltpu.VMEM((ITERS, 7, PAIRS, CHUNK, NV), BF16),
            pltpu.VMEM((ITERS, 7, PAIRS, CHUNK, NV), BF16),
            pltpu.VMEM((PAIRS, CHUNK, NV), BF16),
            pltpu.VMEM((PAIRS, CHUNK, NV), F32),
            dma((ITERS, COPIES)),
            dma((ITERS, COPIES)),
            dma((ITERS, 7)),
            dma((ITERS, 7)),
            dma((ITERS, 7)),
            dma((ITERS, 7)),
            dma((2, 8)),
            dma((3,)),
        ],
        compiler_params=pltpu.CompilerParams(
            collective_id=0, has_side_effects=True, vmem_limit_bytes=60 * 2**20
        ),
        cost_estimate=pl.CostEstimate(
            flops=30_000_000_000, bytes_accessed=40_000_000, transcendentals=0
        ),
        name="ladder",
    )(*args)


def solution(mesh):
    placed = (
        P("kpt", None, None, None),
        P("kpt", None, None, None),
        P("kpt", None, "aux", None, None),
        P("kpt", None, "aux", None, None),
        P(),
        P(),
        P(),
    )
    return jax.shard_map(
        on_device, mesh=mesh, in_specs=placed, out_specs=P("kpt", None, None, None), check_vma=False
    )
```

```python
import functools

import jax
import jax.numpy as jnp
from jax import lax
from jax.experimental import pallas as pl
from jax.experimental.pallas import tpu as pltpu
from jax.sharding import PartitionSpec as P

ITERS = 2
MESH = pl.DeviceIdType.MESH
BF16, F32 = jnp.bfloat16, jnp.float32

NV, PAIRS, NK = 384, 2, 16
LOCAL_AUX = 2
CHUNK = NV // 8
PIECE = NV // 4
HALF = NV // 2

AUX = ((0, 1), (2, 1), (1, 1), (3, 1), (2, 0), (1, 0), (3, 0))
ORDER = ((0, 0), (0, 1), (2, 0), (1, 0), (3, 0), (1, 1), (3, 1), (2, 1))

GROUPS = ITERS * PAIRS

TO_CORE = 0
QUARTER, QUARTER_X, OWN_X, RELAYS, SUMS, ROWS = 8, 9, 10, 11, 12, 13
ALONG_Z = 15
OWN_Y = 17
ARRIVALS = 21


SCHEDULE = {
    0: (("panels", 0), ("clear", 0),),
    1: (("clear", 1),),
    2: (("panels", 1), ("quarter", 0), ("own_x", 0), ("piece0", 0),),
    3: (
        ("panels", 2),
        ("piece1", 0),
        ("quarter_x", 0),
        ("z0", 0),
        ("piece2", 0),
        ("piece3", 0),
        ("begin", 1),
    ),
    4: (("panels", 3),),
    5: (("panels", 4), ("relays", 0),),
    6: (("panels", 5), ("quarter", 1),),
    7: (("panels", 6), ("z1", 0), ("own_x", 1), ("piece0", 1),),
    8: (("panels", 7), ("quarter_x", 1), ("piece1", 1),),
    9: (("scatter", 0), ("piece2", 1),),
    10: (("z0", 1), ("piece3", 1), ("denominators", 0),),
    12: (("relays", 1),),
    13: (("update", 0),),
    14: (("z1", 1),),
    16: (("scatter", 1), ("rows_first", 0), ("rows_rest", 0), ("clear", 2),),
    17: (("quarter", 2), ("piece0", 2), ("update", 1), ("piece1", 2), ("own_x", 2),),
    18: (("quarter_x", 2), ("z0", 2), ("piece2", 2), ("piece3", 2),),
    19: (("rows_first", 1),),
    20: (("rows_rest", 1), ("relays", 2),),
    22: (("z1", 2), ("quarter", 3), ("piece0", 3),),
    23: (("own_x", 3), ("piece1", 3),),
    24: (("scatter", 2), ("clear", 3), ("quarter_x", 3), ("piece2", 3),),
    25: (("z0", 3), ("piece3", 3),),
    28: (("relays", 3),),
    29: (("update", 2),),
    30: (("z1", 3),),
}


def kernel(
    amp_hbm, int_hbm, left_hbm, right_hbm, pair_ref, virt_hbm, cons_hbm,
    out_hbm,
    cur, left, right, own, half, acc, parts_out, parts_in, ints, den, virt, cons,
    sent, recv, load, edge,
):
    kpt, aux = lax.axis_index("kpt"), lax.axis_index("aux")
    y, xl, core = kpt // 4, (kpt // 2) % 2, kpt % 2
    z, xh = aux // 2, aux % 2

    def device(dy=0, dx=0, dc=0, dz=0, dh=0):
        x = (2 * xh + xl + dx + 2 * dh) % 4
        return (
            (((y + dy) % 4) * 2 + x % 2) * 2 + (core + dc) % 2,
            ((z + dz) % 4) * 2 + x // 2,
        )

    def block(dy, dx):
        return (((y + dy) % 4) * 2 + (xl + dx) % 2) * 2 + core

    def rows_of(start, size):
        return pl.ds(start if isinstance(start, int) else pl.multiple_of(start, 16), size)

    partners = [device(dc=1)]
    partners += [device(dy=1), device(dy=3), device(dy=2), device(dx=1), device(dx=3)]
    partners += [device(dz=dz, dh=dh) for dz, dh in AUX]
    barrier = pltpu.get_barrier_semaphore()
    for partner in partners:
        pl.semaphore_signal(barrier, inc=1, device_id=partner, device_id_type=MESH)

    def first_load():
        return pltpu.make_async_copy(amp_hbm.at[0], own.at[0], edge.at[0])

    def ints_load():
        return pltpu.make_async_copy(int_hbm.at[0, :, rows_of(aux * CHUNK, CHUNK)], ints, edge.at[1])

    def step_place(step):
        later = (step + 6) // 8
        dx = (1 - later) * step + later * ((step + 1) // 3 - 1)
        third = (step + 1 + dx) % 3
        dy = later * (2 - third % 2 + third // 2)
        return ((y + dy) % 4) * 2 + (xl + dx) % 2

    def panel_loads(step):
        place = step_place(step) * 2
        return [
            pltpu.make_async_copy(
                source.at[0, pl.ds(place, 2)], target.at[pl.ds(place, 2)], load.at[step, which]
            )
            for which, (source, target) in enumerate(((right_hbm, right), (left_hbm, left)))
        ]

    def small_loads():
        return [
            ints_load(),
            pltpu.make_async_copy(virt_hbm, virt, edge.at[2]),
            pltpu.make_async_copy(cons_hbm.at[0, pl.ds(0, 8)], cons, edge.at[3]),
        ]

    first_load().start()
    for one in small_loads():
        one.start()

    def start_loads(step, unused):
        for one in panel_loads(step):
            one.start()
        return unused

    lax.fori_loop(0, 8, start_loads, 0)

    def denominators():
        for one in small_loads():
            one.wait()
        partner_row = cons[0, kpt]
        energy_b = virt[pl.ds(partner_row, 1), :]
        energy_a = virt[pl.ds(kpt, 1), :]
        row = lax.broadcasted_iota(jnp.int32, (CHUNK, NV), 0) + aux * CHUNK
        lane = lax.broadcasted_iota(jnp.int32, (CHUNK, NV), 1)
        column = jnp.sum(
            jnp.where(row == lane, jnp.broadcast_to(energy_a, (CHUNK, NV)), 0.0),
            axis=1, keepdims=True,
        )
        for p in range(PAIRS):
            den[p] = (pair_ref[p] - column) - energy_b

    first_load().wait()
    pl.semaphore_wait(barrier, len(partners))

    def copy(group, number, place, start, size, target=None, first=False):
        it, p = group // PAIRS, group % PAIRS
        there = cur.at[it, place, p, rows_of(start, size)]
        here = own.at[it, p, rows_of(start, size)] if first else there
        return pltpu.make_async_remote_copy(
            src_ref=here, dst_ref=there,
            send_sem=sent.at[0], recv_sem=recv.at[group, number],
            device_id=device(dc=1) if target is None else target, device_id_type=MESH,
        )

    def arrived(group, number, rows):
        it, p = group // PAIRS, group % PAIRS
        if rows > NV:
            there = cur.at[it, pl.ds(0, rows // NV), p]
        else:
            there = cur.at[it, 0, p, pl.ds(0, rows)]
        pltpu.make_async_copy(there, there, recv.at[group, number]).wait()

    def to_core(group, which):
        return copy(group, TO_CORE + which, block(*ORDER[which]), 0, NV, first=which == 0)

    def quarter(group):
        return copy(group, QUARTER, block(0, 0), z * PIECE, PIECE, device(dy=2), True)

    def quarter_x(group, way):
        start = z * PIECE + way * CHUNK
        return copy(group, QUARTER_X, block(2, 0), start, CHUNK, device(dx=(1, 3)[way]))

    def along_z(group, column, way):
        target = device(dz=(1, 3, 2)[way])
        return copy(group, ALONG_Z + column, block(2, column), z * PIECE, PIECE, target)

    def own_x(group, way):
        return copy(group, OWN_X, block(0, 0), way * HALF, HALF, device(dx=(1, 3)[way]), True)

    def own_y(group, piece, way):
        start = ((z + piece) % 4) * PIECE
        return copy(group, OWN_Y + piece, block(0, 0), start, PIECE, device(dy=(1, 3)[way]), True)

    def relay_x(group, piece, which, way):
        start = ((z + piece) % 4) * PIECE + way * CHUNK
        target = device(dx=(1, 3)[way])
        return copy(group, RELAYS, block((3, 1)[which], 0), start, CHUNK, target)

    def relay_y(group, piece, way):
        start = ((z + piece) % 4) * PIECE
        return copy(group, RELAYS, block(0, 1), start, PIECE, device(dy=(1, 3)[way]))

    def aux_index(o):
        dz, dh = AUX[o]
        return device(dz=dz, dh=dh)[1]

    def rs_copy(group, o):
        dz, dh = AUX[o]
        return pltpu.make_async_remote_copy(
            src_ref=parts_out.at[group, o], dst_ref=parts_in.at[group, o],
            send_sem=sent.at[1], recv_sem=recv.at[group, SUMS],
            device_id=device(dz=dz, dh=dh), device_id_type=MESH,
        )

    def ag_copy(group, o):
        it, p = group // PAIRS, group % PAIRS
        dz, dh = AUX[o]
        rows = rows_of(aux * CHUNK, CHUNK)
        return pltpu.make_async_remote_copy(
            src_ref=own.at[it + 1, p, rows], dst_ref=own.at[it + 1, p, rows],
            send_sem=sent.at[1], recv_sem=recv.at[group, ROWS + min(o, 1)],
            device_id=device(dz=dz, dh=dh), device_id_type=MESH,
        )

    def begin_quarter(group):
        quarter(group).start()
        for way in range(2):
            own_y(group, 0, way).start()

    def begin_rest(group):
        for way in range(2):
            own_x(group, way).start()
        for piece in range(1, 4):
            for way in range(2):
                own_y(group, piece, way).start()

    def share_own(group):
        to_core(group, 0).start()
        it, p = group // PAIRS, group % PAIRS
        cur[it, block(0, 0), p] = own[it, p]

    def take_quarter(group):
        arrived(group, QUARTER, PIECE)
        for way in range(3):
            along_z(group, 0, way).start()
        for way in range(2):
            quarter_x(group, way).start()

    def take_own_x(group):
        arrived(group, OWN_X, NV)
        to_core(group, 1).start()
        for piece in range(2, 4):
            for way in range(2):
                relay_y(group, piece, way).start()

    def take_piece(group, piece):
        arrived(group, OWN_Y + piece, 2 * PIECE)
        if piece < 2:
            for which in range(2):
                for way in range(2):
                    relay_x(group, piece, which, way).start()
        elif piece == 3:
            to_core(group, 3).start()
            to_core(group, 4).start()

    def take_quarter_x(group):
        arrived(group, QUARTER_X, PIECE)
        for way in range(3):
            along_z(group, 1, way).start()

    def take_z(group, column):
        arrived(group, ALONG_Z + column, 3 * PIECE)
        to_core(group, (2, 7)[column]).start()

    def take_relays(group):
        arrived(group, RELAYS, 2 * NV)
        to_core(group, 5).start()
        to_core(group, 6).start()

    def scatter(group):
        p = group % PAIRS
        for o in (1, 2, 3, 4, 0, 5, 6):
            rows = rows_of(aux_index(o) * CHUNK, CHUNK)
            parts_out[group, o] = acc[p, rows].astype(BF16)
            rs_copy(group, o).start()

    def update(group):
        it, p = group // PAIRS, group % PAIRS
        arrived(group, SUMS, 7 * CHUNK)
        rows = rows_of(aux * CHUNK, CHUNK)
        total = acc[p, rows]
        for o in range(7):
            total = total + parts_in[group, o].astype(F32)
        own[it + 1, p, rows] = ((ints[p].astype(F32) + total) / den[p]).astype(BF16)
        for o in range(7):
            ag_copy(group, o).start()

    def take_rows_first(group):
        arrived(group, ROWS, CHUNK)
        if group < GROUPS - PAIRS:
            begin_quarter(group + PAIRS)

    def take_rows_rest(group):
        arrived(group, ROWS + 1, 6 * CHUNK)
        if group < GROUPS - PAIRS:
            share_own(group + PAIRS)
            begin_rest(group + PAIRS)

    def begin(group):
        begin_quarter(group)
        begin_rest(group)

    def clear(group):
        acc[group % PAIRS] = jnp.zeros((NV, NV), F32)

    def take_panels(step):
        for one in panel_loads(step):
            one.wait()

    events = {
        "begin": begin, "quarter": take_quarter, "own_x": take_own_x, "quarter_x": take_quarter_x,
        "relays": take_relays, "update": update, "rows_first": take_rows_first,
        "rows_rest": take_rows_rest, "scatter": scatter, "clear": clear, "panels": take_panels,
        "denominators": lambda group: denominators(),
        "piece0": functools.partial(take_piece, piece=0),
        "piece1": functools.partial(take_piece, piece=1),
        "piece2": functools.partial(take_piece, piece=2),
        "piece3": functools.partial(take_piece, piece=3),
        "z0": functools.partial(take_z, column=0),
        "z1": functools.partial(take_z, column=1),
    }

    def turn(number, unused):
        second = (number + 63) // 64 - (number + 62) // 64
        shifted = (number + 62) // 64 - (number + 55) // 64
        place = number + 7 * second - shifted
        group, step = place // 8, place % 8
        it, p = group // PAIRS, group % PAIRS

        def happen(low, high):
            ticks = [at for at in SCHEDULE if low <= at < high]
            if not ticks:
                return
            if high - low == 1:
                for name, which in SCHEDULE[low]:
                    events[name](which)
                return
            middle = (low + high) // 2
            pl.when(number < middle)(lambda: happen(low, middle))
            pl.when(number >= middle)(lambda: happen(middle, high))

        happen(0, 8 * GROUPS)

        def first_product(i):
            place = step_place(step) * 2 + (core if i == 0 else 1 - core)
            panel = right[place].reshape(LOCAL_AUX * NV, NV)
            product = lax.dot_general(
                cur[it, place, p], panel, (((1,), (1,)), ((), ())), preferred_element_type=F32
            ).astype(BF16)
            for l in range(LOCAL_AUX):
                half[(i * 2 + l) * NV : (i * 2 + l + 1) * NV] = product[:, l * NV : (l + 1) * NV]
            return place

        there = cur.at[it, 0, p]
        pltpu.make_async_copy(there, there, recv.at[group, TO_CORE + step]).wait()
        mine, other = first_product(0), first_product(1)
        panels = jnp.concatenate([left[k, l] for k in (mine, other) for l in range(2)], axis=1)
        acc[p] += jnp.dot(panels, half[...], preferred_element_type=F32)
        return unused

    share_own(0)
    begin(0)
    share_own(1)
    lax.fori_loop(0, 8 * GROUPS, turn, 0)
    scatter(GROUPS - 1)
    take_rows_first(GROUPS - 2)
    take_rows_rest(GROUPS - 2)
    writes = [
        pltpu.make_async_copy(own.at[ITERS, p], out_hbm.at[0, p], edge.at[4 + p])
        for p in range(PAIRS)
    ]
    writes[0].start()
    update(GROUPS - 1)
    take_rows_first(GROUPS - 1)
    take_rows_rest(GROUPS - 1)
    writes[1].start()

    there = cur.at[:, pl.ds(0, 15)]
    pltpu.make_async_copy(there, there, sent.at[0]).wait()
    for back in (parts_out, parts_in):
        pltpu.make_async_copy(back, back, sent.at[1]).wait()
    for one in writes:
        one.wait()


def on_device(*args):
    anywhere = pl.BlockSpec(memory_space=pl.ANY)
    smem = pl.BlockSpec(memory_space=pltpu.SMEM)
    dma = pltpu.SemaphoreType.DMA
    return pl.pallas_call(
        kernel,
        out_shape=jax.ShapeDtypeStruct((1, PAIRS, NV, NV), BF16),
        in_specs=[anywhere] * 4 + [smem, anywhere, anywhere],
        out_specs=anywhere,
        scratch_shapes=[
            pltpu.VMEM((ITERS, NK, PAIRS, NV, NV), BF16),
            pltpu.VMEM((NK, LOCAL_AUX, NV, NV), BF16),
            pltpu.VMEM((NK, LOCAL_AUX, NV, NV), BF16),
            pltpu.VMEM((ITERS + 1, PAIRS, NV, NV), BF16),
            pltpu.VMEM((2 * LOCAL_AUX * NV, NV), BF16),
            pltpu.VMEM((PAIRS, NV, NV), F32),
            pltpu.VMEM((GROUPS, 7, CHUNK, NV), BF16),
            pltpu.VMEM((GROUPS, 7, CHUNK, NV), BF16),
            pltpu.VMEM((PAIRS, CHUNK, NV), BF16),
            pltpu.VMEM((PAIRS, CHUNK, NV), F32),
            pltpu.VMEM((NK, NV), F32),
            pltpu.SMEM((8, NK), jnp.int32),
            dma((2,)),
            dma((GROUPS, ARRIVALS)),
            dma((8, 2)),
            dma((6,)),
        ],
        compiler_params=pltpu.CompilerParams(
            collective_id=0, has_side_effects=True, vmem_limit_bytes=60 * 2**20
        ),
        cost_estimate=pl.CostEstimate(
            flops=30_000_000_000, bytes_accessed=40_000_000, transcendentals=0
        ),
        name="ladder",
    )(*args)


def solution(mesh):
    placed = (
        P("kpt", None, None, None),
        P("kpt", None, None, None),
        P("kpt", None, "aux", None, None),
        P("kpt", None, "aux", None, None),
        P(),
        P(),
        P(),
    )
    return jax.shard_map(
        on_device, mesh=mesh, in_specs=placed, out_specs=P("kpt", None, None, None), check_vma=False
    )
```

```python
import functools

import jax
import jax.numpy as jnp
from jax import lax
from jax.experimental import pallas as pl
from jax.experimental.pallas import tpu as pltpu
from jax.sharding import PartitionSpec as P

ITERS = 2
MESH = pl.DeviceIdType.MESH
BF16, F32 = jnp.bfloat16, jnp.float32

NV, PAIRS, NK = 384, 2, 16
LOCAL_AUX = 2
CHUNK = NV // 8
PIECE = NV // 4
HALF = NV // 2

AUX = ((0, 1), (2, 1), (1, 1), (3, 1), (2, 0), (1, 0), (3, 0))
ORDER = ((0, 0), (0, 1), (2, 0), (1, 0), (3, 0), (1, 1), (3, 1), (2, 1))

GROUPS = ITERS * PAIRS

TO_CORE = 0
QUARTER, QUARTER_X, OWN_X, RELAYS, SUMS, ROWS = 8, 9, 10, 11, 12, 13
ALONG_Z = 15
OWN_Y = 17
ARRIVALS = 21


SCHEDULE = {
    0: (("panels", 0), ("clear", 0),),
    1: (("clear", 1),),
    2: (("panels", 1), ("quarter", 0), ("own_x", 0), ("piece0", 0),),
    3: (
        ("panels", 2),
        ("piece1", 0),
        ("quarter_x", 0),
        ("z0", 0),
        ("piece2", 0),
        ("piece3", 0),
        ("begin", 1),
    ),
    4: (("panels", 3),),
    5: (("panels", 4), ("relays", 0),),
    6: (("panels", 5), ("quarter", 1),),
    7: (("panels", 6), ("z1", 0), ("own_x", 1), ("piece0", 1),),
    8: (("panels", 7), ("quarter_x", 1), ("piece1", 1),),
    9: (("scatter", 0), ("piece2", 1), ("z0", 1),),
    10: (("piece3", 1), ("denominators", 0),),
    12: (("relays", 1),),
    13: (("update", 0),),
    14: (("z1", 1),),
    16: (("scatter", 1), ("rows_first", 0), ("rows_rest", 0), ("clear", 2),),
    17: (("quarter", 2), ("piece0", 2), ("update", 1), ("piece1", 2), ("own_x", 2),),
    18: (("quarter_x", 2), ("z0", 2), ("piece2", 2), ("piece3", 2),),
    19: (("rows_first", 1),),
    20: (("rows_rest", 1), ("relays", 2),),
    22: (("z1", 2), ("quarter", 3), ("piece0", 3),),
    23: (("own_x", 3), ("piece1", 3),),
    24: (("scatter", 2), ("clear", 3), ("quarter_x", 3), ("piece2", 3),),
    25: (("z0", 3), ("piece3", 3),),
    28: (("relays", 3),),
    29: (("update", 2),),
    30: (("z1", 3),),
}


def kernel(
    amp_hbm, int_hbm, left_hbm, right_hbm, pair_hbm, virt_hbm, cons_hbm,
    out_ref,
    cur, left, right, own, half, acc, parts_out, parts_in, ints, den, virt, cons, pair,
    sent, recv, load, edge,
):
    kpt, aux = lax.axis_index("kpt"), lax.axis_index("aux")
    y, xl, core = kpt // 4, (kpt // 2) % 2, kpt % 2
    z, xh = aux // 2, aux % 2

    def device(dy=0, dx=0, dc=0, dz=0, dh=0):
        x = (2 * xh + xl + dx + 2 * dh) % 4
        return (
            (((y + dy) % 4) * 2 + x % 2) * 2 + (core + dc) % 2,
            ((z + dz) % 4) * 2 + x // 2,
        )

    def block(dy, dx):
        return (((y + dy) % 4) * 2 + (xl + dx) % 2) * 2 + core

    def rows_of(start, size):
        return pl.ds(start if isinstance(start, int) else pl.multiple_of(start, 16), size)

    partners = [device(dc=1)]
    partners += [device(dy=1), device(dy=3), device(dy=2), device(dx=1), device(dx=3)]
    partners += [device(dz=dz, dh=dh) for dz, dh in AUX]
    barrier = pltpu.get_barrier_semaphore()
    for partner in partners:
        pl.semaphore_signal(barrier, inc=1, device_id=partner, device_id_type=MESH)

    def first_load(p):
        return pltpu.make_async_copy(amp_hbm.at[0, p], own.at[0, p], edge.at[4 + p])

    def ints_load():
        return pltpu.make_async_copy(int_hbm.at[0, :, rows_of(aux * CHUNK, CHUNK)], ints, edge.at[1])

    def step_place(step):
        later = (step + 6) // 8
        dx = (1 - later) * step + later * ((step + 1) // 3 - 1)
        third = (step + 1 + dx) % 3
        dy = later * (2 - third % 2 + third // 2)
        return ((y + dy) % 4) * 2 + (xl + dx) % 2

    def panel_loads(step):
        place = step_place(step) * 2
        return [
            pltpu.make_async_copy(
                source.at[0, pl.ds(place, 2)], target.at[pl.ds(place, 2)], load.at[step, which]
            )
            for which, (source, target) in enumerate(((right_hbm, right), (left_hbm, left)))
        ]

    def small_loads():
        return [
            ints_load(),
            pltpu.make_async_copy(virt_hbm, virt, edge.at[2]),
            pltpu.make_async_copy(cons_hbm.at[0, pl.ds(0, 8)], cons, edge.at[3]),
            pltpu.make_async_copy(pair_hbm, pair, edge.at[6]),
        ]

    first_load(0).start()
    first_load(1).start()
    for one in small_loads():
        one.start()

    def start_loads(step, unused):
        for one in panel_loads(step):
            one.start()
        return unused

    lax.fori_loop(0, 8, start_loads, 0)

    def denominators():
        for one in small_loads():
            one.wait()
        partner_row = cons[0, kpt]
        energy_b = virt[pl.ds(partner_row, 1), :]
        energy_a = virt[pl.ds(kpt, 1), :]
        row = lax.broadcasted_iota(jnp.int32, (CHUNK, NV), 0) + aux * CHUNK
        lane = lax.broadcasted_iota(jnp.int32, (CHUNK, NV), 1)
        column = jnp.sum(
            jnp.where(row == lane, jnp.broadcast_to(energy_a, (CHUNK, NV)), 0.0),
            axis=1, keepdims=True,
        )
        for p in range(PAIRS):
            den[p] = (pair[p] - column) - energy_b

    first_load(0).wait()
    pl.semaphore_wait(barrier, len(partners))

    def copy(group, number, place, start, size, target=None, first=False):
        it, p = group // PAIRS, group % PAIRS
        there = cur.at[it, place, p, rows_of(start, size)]
        here = own.at[it, p, rows_of(start, size)] if first else there
        return pltpu.make_async_remote_copy(
            src_ref=here, dst_ref=there,
            send_sem=sent.at[0], recv_sem=recv.at[group, number],
            device_id=device(dc=1) if target is None else target, device_id_type=MESH,
        )

    def arrived(group, number, rows):
        it, p = group // PAIRS, group % PAIRS
        if rows > NV:
            there = cur.at[it, pl.ds(0, rows // NV), p]
        else:
            there = cur.at[it, 0, p, pl.ds(0, rows)]
        pltpu.make_async_copy(there, there, recv.at[group, number]).wait()

    def to_core(group, which):
        return copy(group, TO_CORE + which, block(*ORDER[which]), 0, NV, first=which == 0)

    def quarter(group):
        return copy(group, QUARTER, block(0, 0), z * PIECE, PIECE, device(dy=2), True)

    def quarter_x(group, way):
        start = z * PIECE + way * CHUNK
        return copy(group, QUARTER_X, block(2, 0), start, CHUNK, device(dx=(1, 3)[way]))

    def along_z(group, column, way):
        target = device(dz=(1, 3, 2)[way])
        return copy(group, ALONG_Z + column, block(2, column), z * PIECE, PIECE, target)

    def own_x(group, way):
        return copy(group, OWN_X, block(0, 0), way * HALF, HALF, device(dx=(1, 3)[way]), True)

    def own_y(group, piece, way):
        start = ((z + piece) % 4) * PIECE
        return copy(group, OWN_Y + piece, block(0, 0), start, PIECE, device(dy=(1, 3)[way]), True)

    def relay_x(group, piece, which, way):
        start = ((z + piece) % 4) * PIECE + way * CHUNK
        target = device(dx=(1, 3)[way])
        return copy(group, RELAYS, block((3, 1)[which], 0), start, CHUNK, target)

    def relay_y(group, piece, way):
        start = ((z + piece) % 4) * PIECE
        return copy(group, RELAYS, block(0, 1), start, PIECE, device(dy=(1, 3)[way]))

    def aux_index(o):
        dz, dh = AUX[o]
        return device(dz=dz, dh=dh)[1]

    def rs_copy(group, o):
        dz, dh = AUX[o]
        return pltpu.make_async_remote_copy(
            src_ref=parts_out.at[group, o], dst_ref=parts_in.at[group, o],
            send_sem=sent.at[1], recv_sem=recv.at[group, SUMS],
            device_id=device(dz=dz, dh=dh), device_id_type=MESH,
        )

    def ag_copy(group, o):
        it, p = group // PAIRS, group % PAIRS
        dz, dh = AUX[o]
        rows = rows_of(aux * CHUNK, CHUNK)
        there = out_ref.at[0, p, rows] if it == ITERS - 1 else own.at[it + 1, p, rows]
        return pltpu.make_async_remote_copy(
            src_ref=there, dst_ref=there,
            send_sem=sent.at[1], recv_sem=recv.at[group, ROWS + min(o, 1)],
            device_id=device(dz=dz, dh=dh), device_id_type=MESH,
        )

    def begin_quarter(group):
        quarter(group).start()
        for way in range(2):
            own_y(group, 0, way).start()

    def begin_rest(group):
        for way in range(2):
            own_x(group, way).start()
        for piece in range(1, 4):
            for way in range(2):
                own_y(group, piece, way).start()

    def share_own(group):
        to_core(group, 0).start()
        it, p = group // PAIRS, group % PAIRS
        cur[it, block(0, 0), p] = own[it, p]

    def take_quarter(group):
        arrived(group, QUARTER, PIECE)
        for way in range(3):
            along_z(group, 0, way).start()
        for way in range(2):
            quarter_x(group, way).start()

    def take_own_x(group):
        arrived(group, OWN_X, NV)
        to_core(group, 1).start()
        for piece in range(2, 4):
            for way in range(2):
                relay_y(group, piece, way).start()

    def take_piece(group, piece):
        arrived(group, OWN_Y + piece, 2 * PIECE)
        if piece < 2:
            for which in range(2):
                for way in range(2):
                    relay_x(group, piece, which, way).start()
        elif piece == 3:
            to_core(group, 3).start()
            to_core(group, 4).start()

    def take_quarter_x(group):
        arrived(group, QUARTER_X, PIECE)
        for way in range(3):
            along_z(group, 1, way).start()

    def take_z(group, column):
        arrived(group, ALONG_Z + column, 3 * PIECE)
        to_core(group, (2, 7)[column]).start()

    def take_relays(group):
        arrived(group, RELAYS, 2 * NV)
        to_core(group, 5).start()
        to_core(group, 6).start()

    def scatter(group):
        p = group % PAIRS
        for o in (1, 2, 3, 4, 0, 5, 6):
            rows = rows_of(aux_index(o) * CHUNK, CHUNK)
            parts_out[group, o] = acc[p, rows].astype(BF16)
            rs_copy(group, o).start()

    def update(group):
        it, p = group // PAIRS, group % PAIRS
        arrived(group, SUMS, 7 * CHUNK)
        rows = rows_of(aux * CHUNK, CHUNK)
        total = acc[p, rows]
        for o in range(7):
            total = total + parts_in[group, o].astype(F32)
        fresh = ((ints[p].astype(F32) + total) / den[p]).astype(BF16)
        if it == ITERS - 1:
            out_ref[0, p, rows] = fresh
        else:
            own[it + 1, p, rows] = fresh
        for o in range(7):
            ag_copy(group, o).start()

    def take_rows_first(group):
        arrived(group, ROWS, CHUNK)
        if group < GROUPS - PAIRS:
            begin_quarter(group + PAIRS)

    def take_rows_rest(group):
        arrived(group, ROWS + 1, 6 * CHUNK)
        if group < GROUPS - PAIRS:
            share_own(group + PAIRS)
            begin_rest(group + PAIRS)

    def begin(group):
        begin_quarter(group)
        begin_rest(group)

    def clear(group):
        acc[group % PAIRS] = jnp.zeros((NV, NV), F32)

    def take_panels(step):
        for one in panel_loads(step):
            one.wait()

    events = {
        "begin": begin, "quarter": take_quarter, "own_x": take_own_x, "quarter_x": take_quarter_x,
        "relays": take_relays, "update": update, "rows_first": take_rows_first,
        "rows_rest": take_rows_rest, "scatter": scatter, "clear": clear, "panels": take_panels,
        "denominators": lambda group: denominators(),
        "piece0": functools.partial(take_piece, piece=0),
        "piece1": functools.partial(take_piece, piece=1),
        "piece2": functools.partial(take_piece, piece=2),
        "piece3": functools.partial(take_piece, piece=3),
        "z0": functools.partial(take_z, column=0),
        "z1": functools.partial(take_z, column=1),
    }

    def turn(number, unused):
        second = (number + 63) // 64 - (number + 62) // 64
        shifted = (number + 62) // 64 - (number + 55) // 64
        place = number + 7 * second - shifted
        group, step = place // 8, place % 8
        it, p = group // PAIRS, group % PAIRS

        def happen(low, high):
            ticks = [at for at in SCHEDULE if low <= at < high]
            if not ticks:
                return
            if high - low == 1:
                for name, which in SCHEDULE[low]:
                    events[name](which)
                return
            middle = (low + high) // 2
            lax.cond(number < middle, lambda: happen(low, middle), lambda: happen(middle, high))

        happen(0, 8 * GROUPS)

        def first_product(i):
            place = step_place(step) * 2 + (core if i == 0 else 1 - core)
            panel = right[place].reshape(LOCAL_AUX * NV, NV)
            product = lax.dot_general(
                cur[it, place, p], panel, (((1,), (1,)), ((), ())), preferred_element_type=F32
            ).astype(BF16)
            for l in range(LOCAL_AUX):
                half[(i * 2 + l) * NV : (i * 2 + l + 1) * NV] = product[:, l * NV : (l + 1) * NV]
            return place

        there = cur.at[it, 0, p]
        pltpu.make_async_copy(there, there, recv.at[group, TO_CORE + step]).wait()
        mine, other = first_product(0), first_product(1)
        panels = jnp.concatenate([left[k, l] for k in (mine, other) for l in range(2)], axis=1)
        acc[p] += jnp.dot(panels, half[...], preferred_element_type=F32)
        return unused

    share_own(0)
    begin(0)
    first_load(1).wait()
    share_own(1)
    lax.fori_loop(0, 8 * GROUPS, turn, 0)
    scatter(GROUPS - 1)
    take_rows_first(GROUPS - 2)
    take_rows_rest(GROUPS - 2)
    update(GROUPS - 1)
    take_rows_first(GROUPS - 1)
    take_rows_rest(GROUPS - 1)

    there = cur.at[:, pl.ds(0, 15)]
    pltpu.make_async_copy(there, there, sent.at[0]).wait()
    for back in (parts_out, parts_in):
        pltpu.make_async_copy(back, back, sent.at[1]).wait()


def on_device(*args):
    anywhere = pl.BlockSpec(memory_space=pl.ANY)
    dma = pltpu.SemaphoreType.DMA
    return pl.pallas_call(
        kernel,
        out_shape=pltpu.VMEM((1, PAIRS, NV, NV), BF16),
        in_specs=[anywhere] * 7,
        out_specs=pl.BlockSpec(memory_space=pltpu.VMEM),
        scratch_shapes=[
            pltpu.VMEM((ITERS, NK, PAIRS, NV, NV), BF16),
            pltpu.VMEM((NK, LOCAL_AUX, NV, NV), BF16),
            pltpu.VMEM((NK, LOCAL_AUX, NV, NV), BF16),
            pltpu.VMEM((ITERS, PAIRS, NV, NV), BF16),
            pltpu.VMEM((2 * LOCAL_AUX * NV, NV), BF16),
            pltpu.VMEM((PAIRS, NV, NV), F32),
            pltpu.VMEM((GROUPS, 7, CHUNK, NV), BF16),
            pltpu.VMEM((GROUPS, 7, CHUNK, NV), BF16),
            pltpu.VMEM((PAIRS, CHUNK, NV), BF16),
            pltpu.VMEM((PAIRS, CHUNK, NV), F32),
            pltpu.VMEM((NK, NV), F32),
            pltpu.SMEM((8, NK), jnp.int32),
            pltpu.SMEM((PAIRS,), F32),
            dma((2,)),
            dma((GROUPS, ARRIVALS)),
            dma((8, 2)),
            dma((7,)),
        ],
        compiler_params=pltpu.CompilerParams(
            collective_id=0, has_side_effects=True, vmem_limit_bytes=60 * 2**20
        ),
        cost_estimate=pl.CostEstimate(
            flops=30_000_000_000, bytes_accessed=40_000_000, transcendentals=0
        ),
        name="ladder",
    )(*args)


def solution(mesh):
    placed = (
        P("kpt", None, None, None),
        P("kpt", None, None, None),
        P("kpt", None, "aux", None, None),
        P("kpt", None, "aux", None, None),
        P(),
        P(),
        P(),
    )
    return jax.shard_map(
        on_device, mesh=mesh, in_specs=placed, out_specs=P("kpt", None, None, None), check_vma=False
    )
```
